32 devices in a mesh: real: 2 (over x), tx: 16 (over z, y, core).
Axes of the slice: x: 2, y: 2, z: 4, core: 2. Of those that a mesh axis runs over, the one named last changes fastest.
Arguments:
- misfit_source: float32 [512, 2048], P(('real', 'tx')), parts along dimension 0, may hold values from -24 to 24
- storage: float32 [512, 2048], P(('real', 'tx')), parts along dimension 0, may hold values from 0.02 to 0.5
- conduct_x: float32 [512, 2048], P(('real', 'tx')), parts along dimension 0, may hold values from 0.2 to 5
- conduct_y: float32 [512, 2048], P(('real', 'tx')), parts along dimension 0, may hold values from 0.2 to 5
- well_row: int32 [640], P('tx'), may hold values from 0 to 15
- well_col: int32 [640], P('tx'), may hold values from 0 to 1920
- well_owner: int32 [640, 1], P('tx'), may hold values from 0 to 15
- well_slot: int32 [640], P('tx'), may hold values from 0 to 7
- connection: float32 [640, 128], P('tx'), may hold values from 0.1 to 2
Outputs:
- adjoint_head: float32 [512, 2048], P(('real', 'tx')), parts along dimension 0
- plan_grad: float32 [256, 128], P(('real', 'tx')), parts along dimension 0
The draws below stay inside these ranges and needn't reach their ends.
There are 2 independent parts, one for each index of `real`. The reference program is written for one: setup_inputs(seed, part) draws one part's arguments, and reference() takes and returns one part's arrays. A program takes and returns all parts, laid end to end along the dimension named above; an argument that names none is the same for every part. Nothing has to cross between parts.
All inputs are finite; a program needn't handle non-finite values.
Results may differ from the reference program's by a relative error of at most 0.0001.
Values sent between devices are 32-bit elements; how exact they have to be, the bound alone decides.
A program may use at most 64 MiB of HBM per device.

```python
import math
import jax
import jax.numpy as jnp
from jax import lax

CX = 16
NY = 2048
WPD = 40
BLK_DEV = 8
SCREEN = 128
LEVELS = 5
NU = 2
CSW = 16
NX = 256
WELLS = 640
BLOCKS = 128
N_TX = 16


def with_ends(values, stream_key, least, high):
    longest = values.shape.index(max(values.shape))
    spots = []
    for shift in (0, 1):
        where = [jax.random.randint(jax.random.fold_in(stream_key, axis), (), 0, length) for axis, length in enumerate(values.shape)]
        where[longest] = (where[longest] + shift) % values.shape[longest]
        spots.append(tuple(where))
    return values.at[spots[0]].set(least).at[spots[1]].set(high)


def block_levels(own_key, extent, pieces, least, high):
    level = 1.0
    for axis_at, shards_of in pieces:
        draws = jax.random.uniform(jax.random.fold_in(jax.random.fold_in(own_key, 6), axis_at), (shards_of,), jnp.float32, least / len(pieces), high / len(pieces))
        level = level * jnp.repeat(jnp.exp(draws), extent[axis_at] // shards_of).reshape((-1,) + (1,) * (len(extent) - 1 - axis_at))
    return level


def picks_of(key, rows, number_of, top, lift):
    ranking = jax.random.permutation(jax.random.fold_in(key, 1), number_of)
    favour = ranking
    for power in range(3):
        favour = favour * favour // number_of
    favour = favour * lift // number_of
    chance = jax.random.randint(jax.random.fold_in(key, 2), (rows, number_of), 0, 4096) + favour
    sure = jax.random.permutation(jax.random.fold_in(key, 3), rows)[jnp.arange(number_of) % rows]
    chance = jnp.where(jnp.arange(rows)[:, None] == sure[None, :], 1 << 14, chance)
    score = chance * number_of + jnp.arange(number_of)
    return lax.top_k(score.astype(jnp.int32), top)[1].astype(jnp.int32)


def bell_draw(stream_key, extent, spread, most, cuts=(), held_as=jnp.bfloat16):
    array = jax.random.normal(stream_key, extent, jnp.float32) * spread
    if len(cuts) > 0:
        array = block_levels(stream_key, extent, cuts, -0.22, 0.18) * array
    return jnp.clip(array, min=-most, max=most).astype(held_as)


def setup_inputs(seed: int = 0, part: int = 0) -> dict:
    splits = jax.random.split(jax.random.key(seed), 10)
    part_keys = jax.random.split(jax.random.fold_in(splits[9], part), 10)
    return {
        "misfit_source": bell_draw(part_keys[0], (NX, NY), 4.0, 24.0, ((0, 16),), jnp.float32),
        "storage": jnp.clip(jnp.exp(math.log(0.5) - 3.218876 * jax.random.uniform(part_keys[1], (NX, NY), jnp.float32) ** block_levels(part_keys[1], (NX, NY), ((0, 16),), -0.2, 0.2)), 0.02, 0.5),
        "conduct_x": jnp.clip(jnp.exp(math.log(5.0) - 3.218876 * jax.random.uniform(part_keys[2], (NX, NY), jnp.float32) ** block_levels(part_keys[2], (NX, NY), ((0, 16),), -0.2, 0.2)), 0.2, 5.0),
        "conduct_y": jnp.clip(jnp.exp(math.log(5.0) - 3.218876 * jax.random.uniform(part_keys[3], (NX, NY), jnp.float32) ** block_levels(part_keys[3], (NX, NY), ((0, 16),), -0.2, 0.2)), 0.2, 5.0),
        "well_row": with_ends(jax.random.randint(splits[4], (WELLS,), 0, CX), jax.random.fold_in(splits[4], 1), 0, CX - 1).astype(jnp.int32),
        "well_col": with_ends(jax.random.randint(splits[5], (WELLS,), 0, NY - SCREEN + 1), jax.random.fold_in(splits[5], 1), 0, NY - SCREEN).astype(jnp.int32),
        "well_owner": picks_of(splits[6], WELLS, N_TX, 1, 512),
        "well_slot": with_ends(jax.random.randint(splits[7], (WELLS,), 0, BLK_DEV), jax.random.fold_in(splits[7], 1), 0, BLK_DEV - 1).astype(jnp.int32),
        "connection": jnp.clip(jnp.exp(math.log(2.0) - 2.9957323 * jax.random.uniform(splits[8], (WELLS, SCREEN), jnp.float32) ** block_levels(splits[8], (WELLS, SCREEN), ((0, 16),), -0.2, 0.2)), 0.1, 2.0),
    }


omega_damp = 0.8


def coarsen(storage, along_x, along_y):
    rows, cols = storage.shape
    coarse_store = storage.reshape(rows // 2, 2, cols // 2, 2).sum(axis=(1, 3))
    coarse_x = along_x[1::2].reshape(rows // 2, cols // 2, 2).sum(axis=2)
    coarse_y = (along_y[0::2] + along_y[1::2])[:, 1::2]
    return coarse_store, coarse_x, coarse_y


def operators(storage, along_x, below_x, along_y):
    left_y = jnp.pad(along_y[:, :-1], ((0, 0), (1, 0)))
    diagonal = storage + along_x + below_x + along_y + left_y
    return (storage, along_x, below_x, along_y, left_y, diagonal)


def apply_operator(field, padded, ops):
    storage, along_x, below_x, along_y, left_y, diagonal = ops
    upper = padded[2:]
    lower = padded[:-2]
    right_cell = jnp.pad(field[:, 1:], ((0, 0), (0, 1)))
    left_cell = jnp.pad(field[:, :-1], ((0, 0), (1, 0)))
    return (storage * field + along_x * (field - upper) + below_x * (field - lower)
            + along_y * (field - right_cell) + left_y * (field - left_cell))


def smooth(field, source, ops):
    padded = jnp.pad(field, ((1, 1), (0, 0)))
    return field + omega_damp * (source - apply_operator(field, padded, ops)) / ops[5]


def restrict(field):
    rows, cols = field.shape
    return field.reshape(rows // 2, 2, cols // 2, 2).sum(axis=(1, 3))


def prolong(field):
    rows, cols = field.shape
    return jnp.broadcast_to(field[:, None, :, None], (rows, 2, cols, 2)).reshape(rows * 2, cols * 2)


def vcycle(source, hierarchy, depth):
    ops = hierarchy[depth]
    field = jnp.zeros(source.shape, jnp.float32)
    if depth == len(hierarchy) - 1:
        return lax.fori_loop(0, CSW, lambda index, value: smooth(value, source, ops), field)
    for sweep_index in range(NU):
        field = smooth(field, source, ops)
    padded = jnp.pad(field, ((1, 1), (0, 0)))
    coarse_source = restrict(source - apply_operator(field, padded, ops))
    field = field + prolong(vcycle(coarse_source, hierarchy, depth + 1))
    for sweep_index in range(NU):
        field = smooth(field, source, ops)
    return field


def reference(misfit_source, storage, conduct_x, conduct_y, well_row, well_col, well_owner, well_slot, connection):
    hierarchy = []
    store_now, along_x, along_y = storage, conduct_x, conduct_y
    for depth_index in range(LEVELS):
        below_x = jnp.pad(along_x[:-1], ((1, 0), (0, 0)))
        hierarchy.append(operators(store_now, along_x, below_x, along_y))
        if depth_index < LEVELS - 1:
            store_now, along_x, along_y = coarsen(store_now, along_x, along_y)
    adjoint_head = vcycle(misfit_source, hierarchy, 0)
    tiles = jnp.arange(WELLS, dtype=jnp.int32) // WPD
    global_row = (tiles * CX + well_row).astype(jnp.int32)
    picked = adjoint_head[global_row]
    window = jax.vmap(lambda line, start_col: lax.dynamic_slice_in_dim(line, start_col, SCREEN))(picked, well_col.astype(jnp.int32))
    terms = connection * window
    block_ids = (well_owner[:, 0] * BLK_DEV + well_slot).astype(jnp.int32)
    plan_grad = jax.ops.segment_sum(terms, block_ids, num_segments=BLOCKS)
    return adjoint_head, plan_grad
```

```python
import functools

import jax
import jax.numpy as jnp
from jax import lax
from jax.experimental import pallas as pl
from jax.experimental.pallas import tpu as pltpu
from jax.sharding import PartitionSpec as P

BLK_DEV = 8
SCREEN = 128
CSW = 16
OMEGA = 0.8
F32 = jnp.float32


def iota(shape, dim):
    return lax.broadcasted_iota(jnp.int32, shape, dim)


def dot(a, b):
    return lax.dot_general(
        a, b, (((1,), (0,)), ((), ())), precision=lax.Precision.HIGHEST, preferred_element_type=F32
    )


def roll(x, shift, axis):
    shift = shift % x.shape[axis]
    return x if shift == 0 else pltpu.roll(x, shift, axis)


def pair_cols(x, odd_only=False):
    rows, cols = x.shape
    i, j = iota((256, 128), 0), iota((256, 128), 1)
    pick = (i == 2 * j + 1) if odd_only else (i // 2 == j)
    chunks = cols // 256
    stacked = jnp.concatenate([x[:, 256 * c : 256 * c + 256] for c in range(chunks)], axis=0)
    y = dot(stacked, pick.astype(F32))
    return jnp.concatenate([y[rows * c : rows * (c + 1)] for c in range(chunks)], axis=1)


def twice_cols(x):
    rows, cols = x.shape
    i, j = iota((128, 256), 0), iota((128, 256), 1)
    chunks = cols // 128
    stacked = jnp.concatenate([x[:, 128 * c : 128 * c + 128] for c in range(chunks)], axis=0)
    y = dot(stacked, (j // 2 == i).astype(F32))
    return jnp.concatenate([y[rows * c : rows * (c + 1)] for c in range(chunks)], axis=1)


def rows_by(pick, x):
    return dot(pick.astype(F32), x)


def coefficients(s, ax, ay, live, whole=False):
    rows, cols = s.shape
    row, col = iota((rows, cols), 0), iota((rows, cols), 1)
    bx = roll(ax, 1, 0)
    if whole:
        bx = jnp.where(row == 0, 0.0, bx)
    by = jnp.where(col == 0, 0.0, roll(ay, 1, 1))
    diag = s + ax + bx + ay + by
    w = OMEGA / diag
    if live is not None:
        w = jnp.where(live, w, 0.0)
    cu = w * ax
    if whole:
        cu = jnp.where(row == rows - 1, 0.0, cu)
    cr = jnp.where(col == cols - 1, 0.0, w * ay)
    return (w, cu, w * bx, cr, w * by, diag * (1.0 / OMEGA))


def sweep(u, wb, c):
    return (
        (1.0 - OMEGA) * u
        + wb
        + c[1] * roll(u, -1, 0)
        + c[2] * roll(u, 1, 0)
        + c[3] * roll(u, -1, 1)
        + c[4] * roll(u, 1, 1)
    )


def coefficients_split(s, ax, ay):
    rows, cols = s[0].shape
    row, col = iota((rows, cols), 0), iota((rows, cols), 1)
    bx = (jnp.where(row == 0, 0.0, roll(ax[1], 1, 0)), ax[0])
    out = []
    for h in range(2):
        by = jnp.where(col == 0, 0.0, roll(ay[h], 1, 1))
        diag = s[h] + ax[h] + bx[h] + ay[h] + by
        w = OMEGA / diag
        cu = w * ax[h] if h == 0 else jnp.where(row == rows - 1, 0.0, w * ax[h])
        cr = jnp.where(col == cols - 1, 0.0, w * ay[h])
        out.append((w, cu, w * bx[h], cr, w * by, diag * (1.0 / OMEGA)))
    return out


def sweep_split(u, wb, c):
    upper = (u[1], roll(u[0], -1, 0))
    lower = (roll(u[1], 1, 0), u[0])
    return tuple(
        (1.0 - OMEGA) * u[h]
        + wb[h]
        + c[h][1] * upper[h]
        + c[h][2] * lower[h]
        + c[h][3] * roll(u[h], -1, 1)
        + c[h][4] * roll(u[h], 1, 1)
        for h in range(2)
    )


def presmooth(b, c):
    wb = c[0] * b
    u = sweep(wb, wb, c)
    return wb, u, (sweep(u, wb, c) - u) * c[5]


def kernel(
    n, wells,
    b_ref, s_ref, ax_ref, ay_ref, row_ref, col_ref, owner_ref, slot_ref, con_ref,
    out_ref, plan_ref,
    up0, dn0, below0, above0,
    ops1, below_ops1, above_ops1,
    b1, below_b1, above_b1,
    up_u, dn_u, below_u, above_u,
    m2, below_m2, above_m2,
    ops3, b3, all_ops, all_b, full,
    place, partial, got,
    near_send, near_recv, g_send, g_recv,
):
    me = lax.axis_index("tx")
    barrier = pltpu.get_barrier_semaphore()

    def greet(k, carry):
        pl.semaphore_signal(
            barrier, inc=1, device_id={"tx": lax.rem(me + k, n)}, device_id_type=pl.DeviceIdType.MESH
        )
        return carry

    lax.fori_loop(1, n, greet, 0)

    def near(slot, src_up, src_dn, dst_below, dst_above):
        up = pltpu.make_async_remote_copy(
            src_ref=src_up, dst_ref=dst_below, send_sem=near_send.at[slot, 0],
            recv_sem=near_recv.at[slot, 0], device_id={"tx": jnp.maximum(me - 1, 0)},
            device_id_type=pl.DeviceIdType.MESH,
        )
        dn = pltpu.make_async_remote_copy(
            src_ref=src_dn, dst_ref=dst_above, send_sem=near_send.at[slot, 1],
            recv_sem=near_recv.at[slot, 1], device_id={"tx": jnp.minimum(me + 1, n - 1)},
            device_id_type=pl.DeviceIdType.MESH,
        )

        def start():
            @pl.when(me > 0)
            def _():
                up.start()

            @pl.when(me < n - 1)
            def _():
                dn.start()

        def wait():
            @pl.when(me > 0)
            def _():
                up.wait_send()
                dn.wait_recv()

            @pl.when(me < n - 1)
            def _():
                dn.wait_send()
                up.wait_recv()

        return start, wait

    def gather(slot, source, dest):
        def copy(peer, index):
            return pltpu.make_async_remote_copy(
                src_ref=source(peer), dst_ref=dest.at[index], send_sem=g_send.at[slot, peer],
                recv_sem=g_recv.at[slot, index], device_id={"tx": peer},
                device_id_type=pl.DeviceIdType.MESH,
            )

        def start():
            def body(k, carry):
                copy(lax.rem(me + k, n), me).start()
                return carry

            lax.fori_loop(1, n, body, 0)

        def wait():
            def body(k, carry):
                peer = lax.rem(me + k, n)
                copy(peer, peer).wait_recv()
                copy(peer, peer).wait_send()
                return carry

            lax.fori_loop(1, n, body, 0)

        return start, wait

    def spread(w, carry):
        for k, ref in enumerate((row_ref, col_ref, slot_ref)):
            place[k, pl.ds(w, 1), :] = jnp.full((1, 128), ref[w], jnp.int32)
        return carry

    lax.fori_loop(0, wells, spread, 0, unroll=True)

    ny = b_ref.shape[1]
    pos = iota((8, ny), 0)
    b, s, ax, ay = b_ref[...], s_ref[...], ax_ref[...], ay_ref[...]

    s_last = s[8:] + jnp.where(pos == 6, roll(ax[8:], 1, 0), 0.0)
    send_up = jnp.zeros((8, ny), F32)
    send_dn = jnp.zeros((8, ny), F32)
    for k, (first, last) in enumerate(((s[:8], s_last), (ax[:8], ax[8:]), (ay[:8], ay[8:]), (b[:8], b[8:]))):
        here = pos // 2 == k
        send_up = jnp.where(here, roll(first, 2 * k, 0), send_up)
        send_dn = jnp.where(here, roll(last, 2 * k - 6, 0), send_dn)
    up0[...] = send_up
    dn0[...] = send_dn

    pl.semaphore_wait(barrier, n - 1)
    start0, wait0 = near(0, up0, dn0, below0, above0)
    start0()

    pairs = iota((8, 16), 1) // 2 == iota((8, 16), 0)
    odds = iota((8, 16), 1) == 2 * iota((8, 16), 0) + 1
    ops1[0] = rows_by(pairs, pair_cols(s))
    ops1[1] = rows_by(odds, pair_cols(ax))
    ops1[2] = rows_by(pairs, pair_cols(ay, True))
    start1, wait1 = near(1, ops1, ops1, below_ops1, above_ops1)
    start1()

    wait0()
    idx = iota((24, ny), 0)
    live = (idx < 18) | (idx >= 22)
    live &= ~((me == 0) & (idx >= 18))
    live &= ~((me == n - 1) & (idx >= 16) & (idx < 22))
    below, above = below0[...], above0[...]
    full0 = []
    for k, own in enumerate((s, ax, ay, b)):
        tail = jnp.where(pos < 2, roll(below, -2 * k, 0), roll(above, 6 - 2 * k, 0))
        whole0 = jnp.concatenate([own, tail], axis=0)
        full0.append(jnp.where(live, whole0, 1.0 if k == 0 else 0.0))
    c0 = coefficients(full0[0], full0[1], full0[2], live)
    wb0, u0, r0 = presmooth(full0[3], c0)

    b1[...] = rows_by(pairs, pair_cols(r0[:16]))
    start2, wait2 = near(2, b1, b1, below_b1, above_b1)
    start2()
    up_u[...] = u0[0:2]
    dn_u[...] = u0[14:16]
    start3, wait3 = near(3, up_u, dn_u, below_u, above_u)
    start3()

    wait1()
    n1 = ny // 2
    idx = iota((24, n1), 0)
    live = ~((me == 0) & (idx >= 16)) & ~((me == n - 1) & (idx >= 8) & (idx < 16))
    o1 = []
    for k in range(3):
        v = jnp.concatenate([ops1[k], below_ops1[k], above_ops1[k]], axis=0)
        o1.append(jnp.where(live, v, 1.0 if k == 0 else 0.0))
    c1 = coefficients(o1[0], o1[1], o1[2], live)

    out, inn = iota((16, 24), 0), iota((16, 24), 1)
    used = (out < 8) | (out >= 12)
    base = jnp.where(out < 8, 2 * out, 2 * out - 8)
    pairs2 = used & ((inn == base) | (inn == base + 1))
    odds2 = used & (inn == base + 1)
    n2 = ny // 4
    idx = iota((16, n2), 0)
    live2 = ((idx < 8) | (idx >= 12)) & ~((me == 0) & (idx >= 8)) & ~((me == n - 1) & (idx >= 4) & (idx < 12))
    o2 = [
        jnp.where(live2, rows_by(pairs2, pair_cols(o1[0])), 1.0),
        jnp.where(live2, rows_by(odds2, pair_cols(o1[1])), 0.0),
        jnp.where(live2, rows_by(pairs2, pair_cols(o1[2], True)), 0.0),
    ]
    out, inn = iota((8, 16), 0), iota((8, 16), 1)
    pairs3 = (out < 2) & (inn // 2 == out)
    odds3 = (out < 2) & (inn == 2 * out + 1)
    own3 = (
        rows_by(pairs3, pair_cols(o2[0])),
        rows_by(odds3, pair_cols(o2[1])),
        rows_by(pairs3, pair_cols(o2[2], True)),
    )
    for k in range(3):
        ops3[k] = own3[k][0:2]
        all_ops[me, k] = own3[k][0:2]
    start4, wait4 = gather(0, lambda peer: ops3, all_ops)
    start4()
    c2 = coefficients(o2[0], o2[1], o2[2], live2)

    wait2()
    b1e = jnp.where(live, jnp.concatenate([b1[...], below_b1[...], above_b1[...]], axis=0), 0.0)
    wb1, u1, r1 = presmooth(b1e, c1)
    b2 = rows_by(pairs2, pair_cols(r1))
    _, u2, r2 = presmooth(b2, c2)
    b3_own = rows_by(pairs3, pair_cols(r2))[0:2]
    b3[...] = b3_own
    all_b[me] = b3_own
    start5, wait5 = gather(1, lambda peer: b3, all_b)
    start5()
    m2[0] = u2[0:4]
    m2[1] = b2[0:4]
    start6, wait6 = near(4, m2, m2, below_m2, above_m2)
    start6()

    wait4()
    for k in range(3):
        for t in range(n):
            for h in range(2):
                full[k, h, t : t + 1, :] = all_ops[t, k, h : h + 1]
    s3, x3, y3 = ((full[k, 0], full[k, 1]) for k in range(3))
    c3 = coefficients_split(s3, x3, y3)
    s4 = pair_cols(s3[0] + s3[1])
    x4 = pair_cols(x3[1])
    y4 = pair_cols(y3[0] + y3[1], True)
    c4 = coefficients(s4, x4, y4, None, True)

    wait5()
    for t in range(n):
        for h in range(2):
            full[3, h, t : t + 1, :] = all_b[t, h : h + 1]
    wb3 = tuple(c3[h][0] * full[3, h] for h in range(2))
    u3 = sweep_split(wb3, wb3, c3)
    v3 = sweep_split(u3, wb3, c3)
    r3 = (v3[0] - u3[0]) * c3[0][5] + (v3[1] - u3[1]) * c3[1][5]
    wb4 = c4[0] * pair_cols(r3)
    u4 = lax.fori_loop(0, CSW - 1, lambda i, v: sweep(v, wb4, c4), wb4)
    e4 = twice_cols(u4)
    u3 = (u3[0] + e4, u3[1] + e4)
    u3 = sweep_split(sweep_split(u3, wb3, c3), wb3, c3)

    wait6()
    i, j = iota((16, n), 0), iota((16, n), 1)
    glob = 4 * me + jnp.where(i < 8, i, i - 16)
    held = (i < 8) | (i >= 12)
    e3 = rows_by(held & ((glob == 4 * j) | (glob == 4 * j + 1)), twice_cols(u3[0]))
    e3 += rows_by(held & ((glob == 4 * j + 2) | (glob == 4 * j + 3)), twice_cols(u3[1]))
    gap = jnp.zeros((4, n2), F32)
    u2e, b2e = (
        jnp.where(live2, jnp.concatenate([m2[k], below_m2[k], gap, above_m2[k]], axis=0), 0.0)
        for k in range(2)
    )
    wb2 = c2[0] * b2e
    u2 = sweep(sweep(u2e + e3, wb2, c2), wb2, c2)

    i, j = iota((24, 16), 0), iota((24, 16), 1)
    twice2 = j == jnp.where(i < 16, i // 2, i // 2 + 4)
    u1 = u1 + rows_by(twice2, twice_cols(u2))
    u1 = sweep(sweep(u1, wb1, c1), wb1, c1)

    wait3()
    i, j = iota((24, 24), 0), iota((24, 24), 1)
    twice1 = ((i < 18) & (j == i // 2)) | ((i >= 22) & (j == 23))
    bu, au = below_u[...], above_u[...]
    ends = jnp.concatenate([bu, jnp.zeros((4, ny), F32), au], axis=0)
    row24 = iota((24, ny), 0)
    live = (row24 < 18) | (row24 >= 22)
    live &= ~((me == 0) & (row24 >= 18))
    live &= ~((me == n - 1) & (row24 >= 16) & (row24 < 22))
    u0 = jnp.where(live, jnp.concatenate([u0[:16], ends], axis=0), 0.0)
    u0 = u0 + jnp.where(live, rows_by(twice1, twice_cols(u1)), 0.0)
    u0 = sweep(sweep(u0, wb0, c0), wb0, c0)[:16]
    out_ref[...] = u0

    picked = dot((place[0] == iota((wells, 128), 1)).astype(F32)[:, 0:16], u0)
    picked = jnp.concatenate([picked, jnp.zeros((wells, SCREEN), F32)], axis=1)
    col = place[1]
    chunk = ny // 256
    while chunk >= 1:
        width = 128 * (chunk + 1)
        there = jnp.concatenate([(col & (128 * chunk)) != 0] * (chunk + 1), axis=1)
        picked = jnp.where(there, picked[:, 128 * chunk : 128 * chunk + width], picked[:, :width])
        chunk //= 2
    moved = picked
    shift = jnp.concatenate([col, col], axis=1)
    for bit in (1, 2, 4, 8, 16, 32, 64):
        moved = jnp.where((shift & bit) != 0, roll(moved, -bit, 1), moved)
    terms = con_ref[...] * moved[:, :SCREEN]
    block = owner_ref[...] * BLK_DEV + place[2][:, 0:1]
    hot = block == iota((wells, n * BLK_DEV), 1)
    blocks = lax.dot_general(
        hot.astype(F32), terms, (((0,), (0,)), ((), ())), precision=lax.Precision.HIGHEST,
        preferred_element_type=F32,
    )
    partial[...] = blocks.reshape(n, BLK_DEV, SCREEN)
    start7, wait7 = gather(2, lambda peer: partial.at[peer], got)
    start7()
    got[me] = partial[me]
    wait7()
    plan_ref[...] = jnp.sum(got[...], axis=0)


def shards(n, misfit, storage, conduct_x, conduct_y, well_row, well_col, well_owner, well_slot, connection):
    rows, ny = misfit.shape
    wells = well_row.shape[0]
    vmem = pl.BlockSpec(memory_space=pltpu.VMEM)
    smem = pl.BlockSpec(memory_space=pltpu.SMEM)

    def buf(*shape):
        return pltpu.VMEM(shape, F32)

    n1, n2, n3 = ny // 2, ny // 4, ny // 8
    return pl.pallas_call(
        functools.partial(kernel, n, wells),
        out_shape=(
            jax.ShapeDtypeStruct((rows, ny), F32),
            jax.ShapeDtypeStruct((BLK_DEV, SCREEN), F32),
        ),
        in_specs=[vmem, vmem, vmem, vmem, smem, smem, vmem, smem, vmem],
        out_specs=(vmem, vmem),
        scratch_shapes=[
            buf(8, ny), buf(8, ny), buf(8, ny), buf(8, ny),
            buf(3, 8, n1), buf(3, 8, n1), buf(3, 8, n1),
            buf(8, n1), buf(8, n1), buf(8, n1),
            buf(2, ny), buf(2, ny), buf(2, ny), buf(2, ny),
            buf(2, 4, n2), buf(2, 4, n2), buf(2, 4, n2),
            buf(3, 2, n3), buf(2, n3), buf(n, 3, 2, n3), buf(n, 2, n3), buf(4, 2, n, n3),
            pltpu.VMEM((3, wells, 128), jnp.int32),
            buf(n, BLK_DEV, SCREEN), buf(n, BLK_DEV, SCREEN),
            pltpu.SemaphoreType.DMA((5, 2)), pltpu.SemaphoreType.DMA((5, 2)),
            pltpu.SemaphoreType.DMA((3, n)), pltpu.SemaphoreType.DMA((3, n)),
        ],
        compiler_params=pltpu.CompilerParams(
            collective_id=0, has_side_effects=True, vmem_limit_bytes=40 * 1024 * 1024
        ),
        name="vcycle",
    )(misfit, storage, conduct_x, conduct_y, well_row, well_col, well_owner, well_slot, connection)


def solution(mesh):
    tiles = P(("real", "tx"), None)
    return jax.shard_map(
        functools.partial(shards, mesh.shape["tx"]),
        mesh=mesh,
        in_specs=(tiles, tiles, tiles, tiles, P("tx"), P("tx"), P("tx", None), P("tx"), P("tx", None)),
        out_specs=(tiles, tiles),
        check_vma=False,
    )
```

```python
import functools

import jax
import jax.numpy as jnp
from jax import lax
from jax.experimental import pallas as pl
from jax.experimental.pallas import tpu as pltpu
from jax.sharding import PartitionSpec as P

BLK_DEV = 8
SCREEN = 128
CSW = 16
OMEGA = 0.8
F32 = jnp.float32


def iota(shape, dim):
    return lax.broadcasted_iota(jnp.int32, shape, dim)


def dot(a, b):
    return lax.dot_general(
        a, b, (((1,), (0,)), ((), ())), precision=lax.Precision.HIGHEST, preferred_element_type=F32
    )


def two_parts(x):
    high = x.astype(jnp.bfloat16).astype(F32)
    return jnp.concatenate([high, x - high], axis=0).astype(jnp.bfloat16)


def short_dot(a, b):
    return lax.dot_general(a, b, (((1,), (0,)), ((), ())), preferred_element_type=F32)


def by_pick(x, pick):
    y = short_dot(two_parts(x), pick.astype(F32).astype(jnp.bfloat16))
    return y[: x.shape[0]] + y[x.shape[0] :]


def roll(x, shift, axis):
    shift = shift % x.shape[axis]
    return x if shift == 0 else pltpu.roll(x, shift, axis)


def pair_cols(x, odd_only=False):
    rows, cols = x.shape
    i, j = iota((256, 128), 0), iota((256, 128), 1)
    pick = (i == 2 * j + 1) if odd_only else (i // 2 == j)
    chunks = cols // 256
    stacked = jnp.concatenate([x[:, 256 * c : 256 * c + 256] for c in range(chunks)], axis=0)
    y = by_pick(stacked, pick)
    return jnp.concatenate([y[rows * c : rows * (c + 1)] for c in range(chunks)], axis=1)


def twice_cols(x):
    rows, cols = x.shape
    i, j = iota((128, 256), 0), iota((128, 256), 1)
    chunks = cols // 128
    stacked = jnp.concatenate([x[:, 128 * c : 128 * c + 128] for c in range(chunks)], axis=0)
    y = by_pick(stacked, j // 2 == i)
    return jnp.concatenate([y[rows * c : rows * (c + 1)] for c in range(chunks)], axis=1)


def rows_by(pick, x):
    pick = pick.astype(F32)
    return short_dot(jnp.concatenate([pick, pick], axis=1).astype(jnp.bfloat16), two_parts(x))


def coefficients(s, ax, ay, live, whole=False):
    rows, cols = s.shape
    row, col = iota((rows, cols), 0), iota((rows, cols), 1)
    bx = roll(ax, 1, 0)
    if whole:
        bx = jnp.where(row == 0, 0.0, bx)
    by = jnp.where(col == 0, 0.0, roll(ay, 1, 1))
    diag = s + ax + bx + ay + by
    w = OMEGA / diag
    if live is not None:
        w = jnp.where(live, w, 0.0)
    cu = w * ax
    if whole:
        cu = jnp.where(row == rows - 1, 0.0, cu)
    cr = jnp.where(col == cols - 1, 0.0, w * ay)
    return (w, cu, w * bx, cr, w * by, diag * (1.0 / OMEGA))


def sweep(u, wb, c):
    return (
        (1.0 - OMEGA) * u
        + wb
        + c[1] * roll(u, -1, 0)
        + c[2] * roll(u, 1, 0)
        + c[3] * roll(u, -1, 1)
        + c[4] * roll(u, 1, 1)
    )


def coefficients_split(s, ax, ay):
    rows, cols = s[0].shape
    row, col = iota((rows, cols), 0), iota((rows, cols), 1)
    bx = (jnp.where(row == 0, 0.0, roll(ax[1], 1, 0)), ax[0])
    out = []
    for h in range(2):
        by = jnp.where(col == 0, 0.0, roll(ay[h], 1, 1))
        diag = s[h] + ax[h] + bx[h] + ay[h] + by
        w = OMEGA / diag
        cu = w * ax[h] if h == 0 else jnp.where(row == rows - 1, 0.0, w * ax[h])
        cr = jnp.where(col == cols - 1, 0.0, w * ay[h])
        out.append((w, cu, w * bx[h], cr, w * by, diag * (1.0 / OMEGA)))
    return out


def sweep_split(u, wb, c):
    upper = (u[1], roll(u[0], -1, 0))
    lower = (roll(u[1], 1, 0), u[0])
    return tuple(
        (1.0 - OMEGA) * u[h]
        + wb[h]
        + c[h][1] * upper[h]
        + c[h][2] * lower[h]
        + c[h][3] * roll(u[h], -1, 1)
        + c[h][4] * roll(u[h], 1, 1)
        for h in range(2)
    )


def presmooth(b, c):
    wb = c[0] * b
    u = sweep(wb, wb, c)
    return wb, u, (sweep(u, wb, c) - u) * c[5]


def kernel(
    n, wells,
    b_hbm, s_hbm, ax_hbm, ay_hbm, row_ref, col_ref, owner_ref, slot_ref, con_hbm,
    out_ref, plan_ref,
    b_ref, s_ref, ax_ref, ay_ref, con_ref, up0, dn0, below0, above0,
    ops1, below_ops1, above_ops1,
    b1, below_b1, above_b1,
    up_u, dn_u, below_u, above_u,
    m2, below_m2, above_m2,
    ops3, b3, all_ops, all_b, full,
    place, partial, got,
    near_send, near_recv, g_send, g_recv, in_sem,
):
    me = lax.axis_index("tx")
    loads = [
        pltpu.make_async_copy(src, dst, in_sem.at[k])
        for k, (src, dst) in enumerate(
            ((s_hbm, s_ref), (ax_hbm, ax_ref), (ay_hbm, ay_ref), (b_hbm, b_ref), (con_hbm, con_ref))
        )
    ]
    for load in loads:
        load.start()
    barrier = pltpu.get_barrier_semaphore()

    def greet(k, carry):
        pl.semaphore_signal(
            barrier, inc=1, device_id={"tx": lax.rem(me + k, n)}, device_id_type=pl.DeviceIdType.MESH
        )
        return carry

    lax.fori_loop(1, n, greet, 0)

    def near(slot, src_up, src_dn, dst_below, dst_above):
        up = pltpu.make_async_remote_copy(
            src_ref=src_up, dst_ref=dst_below, send_sem=near_send.at[slot, 0],
            recv_sem=near_recv.at[slot, 0], device_id={"tx": jnp.maximum(me - 1, 0)},
            device_id_type=pl.DeviceIdType.MESH,
        )
        dn = pltpu.make_async_remote_copy(
            src_ref=src_dn, dst_ref=dst_above, send_sem=near_send.at[slot, 1],
            recv_sem=near_recv.at[slot, 1], device_id={"tx": jnp.minimum(me + 1, n - 1)},
            device_id_type=pl.DeviceIdType.MESH,
        )

        def start():
            @pl.when(me > 0)
            def _():
                up.start()

            @pl.when(me < n - 1)
            def _():
                dn.start()

        def wait():
            @pl.when(me > 0)
            def _():
                up.wait_send()
                dn.wait_recv()

            @pl.when(me < n - 1)
            def _():
                dn.wait_send()
                up.wait_recv()

        return start, wait

    def gather(slot, source, dest):
        def copy(peer, index):
            return pltpu.make_async_remote_copy(
                src_ref=source(peer), dst_ref=dest.at[index], send_sem=g_send.at[slot, peer],
                recv_sem=g_recv.at[slot, index], device_id={"tx": peer},
                device_id_type=pl.DeviceIdType.MESH,
            )

        def start():
            def body(k, carry):
                copy(lax.rem(me + k, n), me).start()
                return carry

            lax.fori_loop(1, n, body, 0)

        def wait():
            def body(k, carry):
                peer = lax.rem(me + k, n)
                copy(peer, peer).wait_recv()
                copy(peer, peer).wait_send()
                return carry

            lax.fori_loop(1, n, body, 0)

        return start, wait

    def spread(w, carry):
        for k, ref in enumerate((row_ref, col_ref, slot_ref, owner_ref)):
            place[k, pl.ds(w, 1), :] = jnp.full((1, 128), ref[w], jnp.int32)
        return carry

    lax.fori_loop(0, wells, spread, 0, unroll=True)

    ny = b_ref.shape[1]
    pos = iota((8, ny), 0)
    for load in loads[:4]:
        load.wait()
    b, s, ax, ay = b_ref[...], s_ref[...], ax_ref[...], ay_ref[...]

    s_last = s[8:] + jnp.where(pos == 6, roll(ax[8:], 1, 0), 0.0)
    send_up = jnp.zeros((8, ny), F32)
    send_dn = jnp.zeros((8, ny), F32)
    for k, (first, last) in enumerate(((s[:8], s_last), (ax[:8], ax[8:]), (ay[:8], ay[8:]), (b[:8], b[8:]))):
        here = pos // 2 == k
        send_up = jnp.where(here, roll(first, 2 * k, 0), send_up)
        send_dn = jnp.where(here, roll(last, 2 * k - 6, 0), send_dn)
    up0[...] = send_up
    dn0[...] = send_dn

    pl.semaphore_wait(barrier, n - 1)
    start0, wait0 = near(0, up0, dn0, below0, above0)
    start0()

    pairs = iota((8, 16), 1) // 2 == iota((8, 16), 0)
    odds = iota((8, 16), 1) == 2 * iota((8, 16), 0) + 1
    ops1[0] = rows_by(pairs, pair_cols(s))
    ops1[1] = rows_by(odds, pair_cols(ax))
    ops1[2] = rows_by(pairs, pair_cols(ay, True))
    start1, wait1 = near(1, ops1, ops1, below_ops1, above_ops1)
    start1()

    wait0()
    idx = iota((24, ny), 0)
    live = (idx < 18) | (idx >= 22)
    live &= ~((me == 0) & (idx >= 18))
    live &= ~((me == n - 1) & (idx >= 16) & (idx < 22))
    below, above = below0[...], above0[...]
    full0 = []
    for k, own in enumerate((s, ax, ay, b)):
        tail = jnp.where(pos < 2, roll(below, -2 * k, 0), roll(above, 6 - 2 * k, 0))
        whole0 = jnp.concatenate([own, tail], axis=0)
        full0.append(jnp.where(live, whole0, 1.0 if k == 0 else 0.0))
    c0 = coefficients(full0[0], full0[1], full0[2], live)
    wb0, u0, r0 = presmooth(full0[3], c0)

    b1[...] = rows_by(pairs, pair_cols(r0[:16]))
    start2, wait2 = near(2, b1, b1, below_b1, above_b1)
    start2()
    up_u[...] = u0[0:2]
    dn_u[...] = u0[14:16]
    start3, wait3 = near(3, up_u, dn_u, below_u, above_u)
    start3()

    wait1()
    n1 = ny // 2
    idx = iota((24, n1), 0)
    live = ~((me == 0) & (idx >= 16)) & ~((me == n - 1) & (idx >= 8) & (idx < 16))
    o1 = []
    for k in range(3):
        v = jnp.concatenate([ops1[k], below_ops1[k], above_ops1[k]], axis=0)
        o1.append(jnp.where(live, v, 1.0 if k == 0 else 0.0))
    c1 = coefficients(o1[0], o1[1], o1[2], live)

    out, inn = iota((16, 24), 0), iota((16, 24), 1)
    used = (out < 8) | (out >= 12)
    base = jnp.where(out < 8, 2 * out, 2 * out - 8)
    pairs2 = used & ((inn == base) | (inn == base + 1))
    odds2 = used & (inn == base + 1)
    n2 = ny // 4
    idx = iota((16, n2), 0)
    live2 = ((idx < 8) | (idx >= 12)) & ~((me == 0) & (idx >= 8)) & ~((me == n - 1) & (idx >= 4) & (idx < 12))
    o2 = [
        jnp.where(live2, rows_by(pairs2, pair_cols(o1[0])), 1.0),
        jnp.where(live2, rows_by(odds2, pair_cols(o1[1])), 0.0),
        jnp.where(live2, rows_by(pairs2, pair_cols(o1[2], True)), 0.0),
    ]
    out, inn = iota((8, 16), 0), iota((8, 16), 1)
    pairs3 = (out < 2) & (inn // 2 == out)
    odds3 = (out < 2) & (inn == 2 * out + 1)
    own3 = (
        rows_by(pairs3, pair_cols(o2[0])),
        rows_by(odds3, pair_cols(o2[1])),
        rows_by(pairs3, pair_cols(o2[2], True)),
    )
    for k in range(3):
        ops3[k] = own3[k][0:2]
        all_ops[me, k] = own3[k][0:2]
    start4, wait4 = gather(0, lambda peer: ops3, all_ops)
    start4()
    c2 = coefficients(o2[0], o2[1], o2[2], live2)

    wait2()
    b1e = jnp.where(live, jnp.concatenate([b1[...], below_b1[...], above_b1[...]], axis=0), 0.0)
    wb1, u1, r1 = presmooth(b1e, c1)
    b2 = rows_by(pairs2, pair_cols(r1))
    _, u2, r2 = presmooth(b2, c2)
    b3_own = rows_by(pairs3, pair_cols(r2))[0:2]
    b3[...] = b3_own
    all_b[me] = b3_own
    start5, wait5 = gather(1, lambda peer: b3, all_b)
    start5()
    m2[0] = u2[0:4]
    m2[1] = b2[0:4]
    start6, wait6 = near(4, m2, m2, below_m2, above_m2)
    start6()

    wait4()
    for k in range(3):
        for t in range(n):
            for h in range(2):
                full[k, h, t : t + 1, :] = all_ops[t, k, h : h + 1]
    s3, x3, y3 = ((full[k, 0], full[k, 1]) for k in range(3))
    c3 = coefficients_split(s3, x3, y3)
    s4 = pair_cols(s3[0] + s3[1])
    x4 = pair_cols(x3[1])
    y4 = pair_cols(y3[0] + y3[1], True)
    c4 = coefficients(s4, x4, y4, None, True)

    wait5()
    for t in range(n):
        for h in range(2):
            full[3, h, t : t + 1, :] = all_b[t, h : h + 1]
    wb3 = tuple(c3[h][0] * full[3, h] for h in range(2))
    u3 = sweep_split(wb3, wb3, c3)
    v3 = sweep_split(u3, wb3, c3)
    r3 = (v3[0] - u3[0]) * c3[0][5] + (v3[1] - u3[1]) * c3[1][5]
    wb4 = c4[0] * pair_cols(r3)
    u4 = lax.fori_loop(0, CSW - 1, lambda i, v: sweep(v, wb4, c4), wb4)
    e4 = twice_cols(u4)
    u3 = (u3[0] + e4, u3[1] + e4)
    u3 = sweep_split(sweep_split(u3, wb3, c3), wb3, c3)

    wait6()
    i, j = iota((16, n), 0), iota((16, n), 1)
    glob = 4 * me + jnp.where(i < 8, i, i - 16)
    held = (i < 8) | (i >= 12)
    e3 = rows_by(held & ((glob == 4 * j) | (glob == 4 * j + 1)), twice_cols(u3[0]))
    e3 += rows_by(held & ((glob == 4 * j + 2) | (glob == 4 * j + 3)), twice_cols(u3[1]))
    gap = jnp.zeros((4, n2), F32)
    u2e, b2e = (
        jnp.where(live2, jnp.concatenate([m2[k], below_m2[k], gap, above_m2[k]], axis=0), 0.0)
        for k in range(2)
    )
    wb2 = c2[0] * b2e
    u2 = sweep(sweep(u2e + e3, wb2, c2), wb2, c2)

    i, j = iota((24, 16), 0), iota((24, 16), 1)
    twice2 = j == jnp.where(i < 16, i // 2, i // 2 + 4)
    u1 = u1 + rows_by(twice2, twice_cols(u2))
    u1 = sweep(sweep(u1, wb1, c1), wb1, c1)

    wait3()
    i, j = iota((24, 24), 0), iota((24, 24), 1)
    twice1 = ((i < 18) & (j == i // 2)) | ((i >= 22) & (j == 23))
    bu, au = below_u[...], above_u[...]
    ends = jnp.concatenate([bu, jnp.zeros((4, ny), F32), au], axis=0)
    row24 = iota((24, ny), 0)
    live = (row24 < 18) | (row24 >= 22)
    live &= ~((me == 0) & (row24 >= 18))
    live &= ~((me == n - 1) & (row24 >= 16) & (row24 < 22))
    u0 = jnp.where(live, jnp.concatenate([u0[:16], ends], axis=0), 0.0)
    u0 = u0 + jnp.where(live, rows_by(twice1, twice_cols(u1)), 0.0)
    u0 = sweep(sweep(u0, wb0, c0), wb0, c0)[:16]
    out_ref[...] = u0

    picked = dot((place[0] == iota((wells, 128), 1)).astype(F32)[:, 0:16], u0)
    picked = jnp.concatenate([picked, jnp.zeros((wells, SCREEN), F32)], axis=1)
    col = place[1]
    chunk = ny // 256
    while chunk >= 1:
        width = 128 * (chunk + 1)
        there = jnp.concatenate([(col & (128 * chunk)) != 0] * (chunk + 1), axis=1)
        picked = jnp.where(there, picked[:, 128 * chunk : 128 * chunk + width], picked[:, :width])
        chunk //= 2
    moved = picked
    shift = jnp.concatenate([col, col], axis=1)
    for bit in (1, 2, 4, 8, 16, 32, 64):
        moved = jnp.where((shift & bit) != 0, roll(moved, -bit, 1), moved)
    loads[4].wait()
    terms = con_ref[...] * moved[:, :SCREEN]
    block = (place[3] * BLK_DEV + place[2])[:, 0:1]
    hot = block == iota((wells, n * BLK_DEV), 1)
    blocks = lax.dot_general(
        hot.astype(F32), terms, (((0,), (0,)), ((), ())), precision=lax.Precision.HIGHEST,
        preferred_element_type=F32,
    )
    partial[...] = blocks.reshape(n, BLK_DEV, SCREEN)
    start7, wait7 = gather(2, lambda peer: partial.at[peer], got)
    start7()
    got[me] = partial[me]
    wait7()
    plan_ref[...] = jnp.sum(got[...], axis=0)


def shards(n, misfit, storage, conduct_x, conduct_y, well_row, well_col, well_owner, well_slot, connection):
    rows, ny = misfit.shape
    wells = well_row.shape[0]
    vmem = pl.BlockSpec(memory_space=pltpu.VMEM)
    hbm = pl.BlockSpec(memory_space=pl.ANY)
    smem = pl.BlockSpec(memory_space=pltpu.SMEM)

    def buf(*shape):
        return pltpu.VMEM(shape, F32)

    n1, n2, n3 = ny // 2, ny // 4, ny // 8
    return pl.pallas_call(
        functools.partial(kernel, n, wells),
        out_shape=(
            jax.ShapeDtypeStruct((rows, ny), F32),
            jax.ShapeDtypeStruct((BLK_DEV, SCREEN), F32),
        ),
        in_specs=[hbm, hbm, hbm, hbm, smem, smem, smem, smem, hbm],
        out_specs=(vmem, vmem),
        scratch_shapes=[
            buf(rows, ny), buf(rows, ny), buf(rows, ny), buf(rows, ny), buf(wells, SCREEN),
            buf(8, ny), buf(8, ny), buf(8, ny), buf(8, ny),
            buf(3, 8, n1), buf(3, 8, n1), buf(3, 8, n1),
            buf(8, n1), buf(8, n1), buf(8, n1),
            buf(2, ny), buf(2, ny), buf(2, ny), buf(2, ny),
            buf(2, 4, n2), buf(2, 4, n2), buf(2, 4, n2),
            buf(3, 2, n3), buf(2, n3), buf(n, 3, 2, n3), buf(n, 2, n3), buf(4, 2, n, n3),
            pltpu.VMEM((4, wells, 128), jnp.int32),
            buf(n, BLK_DEV, SCREEN), buf(n, BLK_DEV, SCREEN),
            pltpu.SemaphoreType.DMA((5, 2)), pltpu.SemaphoreType.DMA((5, 2)),
            pltpu.SemaphoreType.DMA((3, n)), pltpu.SemaphoreType.DMA((3, n)),
            pltpu.SemaphoreType.DMA((5,)),
        ],
        compiler_params=pltpu.CompilerParams(
            collective_id=0, has_side_effects=True, vmem_limit_bytes=56 * 1024 * 1024
        ),
        name="vcycle",
    )(misfit, storage, conduct_x, conduct_y, well_row, well_col, well_owner.reshape(wells), well_slot, connection)


def solution(mesh):
    tiles = P(("real", "tx"), None)
    return jax.shard_map(
        functools.partial(shards, mesh.shape["tx"]),
        mesh=mesh,
        in_specs=(tiles, tiles, tiles, tiles, P("tx"), P("tx"), P("tx", None), P("tx"), P("tx", None)),
        out_specs=(tiles, tiles),
        check_vma=False,
    )
```
